32 devices in a mesh: seq: 32 (over z, y, x, core).
Axes of the slice: x: 2, y: 2, z: 4, core: 2. Of those that a mesh axis runs over, the one named last changes fastest.
Arguments:
- signal: bfloat16 [32768, 512], P('seq'), may hold values from -6 to 6
- grad_out: bfloat16 [32768, 512], P('seq'), may hold values from -6 to 6
- conv_weight: bfloat16 [1024, 1024], replicated, may hold values from -0.1875 to 0.1875
- proj_weight: bfloat16 [512, 512], replicated, may hold values from -0.25 to 0.25
Outputs:
- saliency: float32 [32768, 512], P('seq')
The draws below stay inside these ranges and needn't reach their ends.
All inputs are finite; a program needn't handle non-finite values.
Results may differ from the reference program's by a relative error of at most 0.0013.
Values may be sent and summed in bfloat16 or wider, within the bound.
A program may use at most 64 MiB of HBM per device.

```python
import jax
import jax.numpy as jnp
from jax import lax

C = 512
GATE = 1024
TOTAL = 32768
DILATION = 2048


def shard_levels(rng, extent, pieces, smallest, largest):
    def one(axis_at, blocks):
        steps = jax.random.uniform(jax.random.fold_in(jax.random.fold_in(rng, 6), axis_at), (blocks,), jnp.float32, smallest / len(pieces), largest / len(pieces))
        return jnp.repeat(jnp.exp(steps), extent[axis_at] // blocks).reshape((-1,) + (1,) * (len(extent) - axis_at - 1))

    gain = one(*pieces[0])
    for cut in pieces[1:]:
        gain = gain * one(*cut)
    return gain


def bell_draw(own_key, dims, width, limit, pieces=(), dtype=jnp.bfloat16):
    gain = shard_levels(own_key, dims, pieces, -0.22, 0.18) if pieces else 1.0
    entries = jax.random.normal(own_key, dims, jnp.float32) * width * gain
    return jnp.minimum(jnp.maximum(entries, -limit), limit).astype(dtype)


def setup_inputs(seed: int = 0) -> dict:
    keys = jax.random.split(jax.random.key(seed), 5)
    signal = bell_draw(keys[0], (TOTAL, C), 1.0, 6.0, ((0, 32),))
    grad_out = bell_draw(keys[1], (TOTAL, C), 1.0, 6.0, ((0, 32),))
    conv_weight = bell_draw(keys[2], (2 * C, GATE), (2 * C) ** -0.5, 0.1875)
    proj_weight = bell_draw(keys[3], (C, C), C ** -0.5, 0.25)
    return {"signal": signal, "grad_out": grad_out, "conv_weight": conv_weight, "proj_weight": proj_weight}


def contract_rows(left, right):
    return lax.dot_general(left, right, (((1,), (1,)), ((), ())), preferred_element_type=jnp.float32)


def reference(signal, grad_out, conv_weight, proj_weight):
    w_past = conv_weight[:C]
    w_now = conv_weight[C:]
    past = jnp.concatenate([jnp.zeros((DILATION, C), jnp.bfloat16), signal[:-DILATION]], 0)
    gates = jnp.dot(past, w_past, preferred_element_type=jnp.float32) + jnp.dot(signal, w_now, preferred_element_type=jnp.float32)
    tanh_part = jnp.tanh(gates[:, :C])
    sig_part = jax.nn.sigmoid(gates[:, C:])
    d_mixed = contract_rows(grad_out, proj_weight)
    d_tanh = d_mixed * sig_part * (1.0 - tanh_part * tanh_part)
    d_sig = d_mixed * tanh_part * sig_part * (1.0 - sig_part)
    d_gates = jnp.concatenate([d_tanh, d_sig], 1).astype(jnp.bfloat16)
    near = contract_rows(d_gates, w_now)
    far = lax.optimization_barrier(contract_rows(d_gates, w_past).astype(jnp.bfloat16))
    back = jnp.concatenate([far[DILATION:], jnp.zeros((DILATION, C), jnp.bfloat16)], 0).astype(jnp.float32)
    return grad_out.astype(jnp.float32) + near + back
```

```python
import functools

import jax
import jax.numpy as jnp
from jax import lax
from jax.experimental import pallas as pl
from jax.experimental.pallas import tpu as pltpu
from jax.sharding import PartitionSpec as P

MESH = pl.DeviceIdType.MESH
STEPS = 4


def contract_rows(left, right):
    return lax.dot_general(
        left, right, (((1,), (1,)), ((), ())), preferred_element_type=jnp.float32
    )


def kernel(
    devices, steps,
    signal_ref, grad_ref, conv_ref, proj_ref, out_ref,
    feat, grad, grad_home, past, far_in, far_out, sum_in, sum_out, near_b, held,
    conv, proj,
    load_sem, feat_send, feat_recv, grad_send, grad_recv, past_send, past_recv,
    far_send, far_recv, sum_send, sum_recv, store_sem,
):
    me = lax.axis_index("seq")
    odd = lax.rem(lax.div(me, 2), 2)
    partner = me + 2 - 4 * odd
    behind, ahead = me - 4, me + 4
    has_behind, has_ahead = me >= 4, me < devices - 4
    is_odd, is_even = odd == 1, odd == 0
    half, width = feat.shape[1:]
    rows = half // steps
    mine, theirs = odd * half, (1 - odd) * half

    def part(step, base=0):
        return pl.ds(pl.multiple_of(base + step * rows, rows), rows)

    def remote(src, dst, send, recv, target):
        return pltpu.make_async_remote_copy(
            src_ref=src, dst_ref=dst, send_sem=send, recv_sem=recv,
            device_id=(target,), device_id_type=MESH,
        )

    def feat_copy(step, slot):
        return remote(
            signal_ref.at[part(step, theirs)], feat.at[slot, part(step)],
            feat_send.at[step], feat_recv.at[step], partner,
        )

    def grad_copy(step, slot):
        return remote(
            grad_ref.at[part(step, theirs)], grad.at[slot, part(step)],
            grad_send.at[step], grad_recv.at[step], partner,
        )

    def past_copy_own(step):
        return remote(
            signal_ref.at[part(step, mine)], past.at[part(step)],
            past_send.at[step], past_recv.at[step], ahead,
        )

    def past_copy_on(step):
        return remote(
            feat.at[1, part(step)], past.at[part(step)],
            past_send.at[step], past_recv.at[step], ahead,
        )

    def far_copy(step):
        return remote(
            far_out.at[part(step)], far_in.at[part(step)],
            far_send.at[step], far_recv.at[step], behind,
        )

    def sum_copy(step):
        return remote(
            sum_out.at[part(step)], sum_in.at[part(step)],
            sum_send.at[step], sum_recv.at[step], partner,
        )

    def store(step, base, index):
        return pltpu.make_async_copy(
            held.at[part(step, base)], out_ref.at[part(step, base)],
            store_sem.at[index],
        )

    loads = [
        pltpu.make_async_copy(src, dst, load_sem.at[i])
        for i, (src, dst) in enumerate([
            (conv_ref, conv),
            (proj_ref, proj),
            (signal_ref.at[pl.ds(pl.multiple_of(mine, half), half)], feat.at[odd]),
            (grad_ref.at[pl.ds(pl.multiple_of(mine, half), half)], grad.at[odd]),
            (grad_ref.at[pl.ds(pl.multiple_of(theirs, half), half)], grad_home),
        ])
    ]

    barrier = pltpu.get_barrier_semaphore()
    pl.semaphore_signal(barrier, inc=1, device_id=(partner,), device_id_type=MESH)

    @pl.when(has_behind)
    def _():
        pl.semaphore_signal(barrier, inc=1, device_id=(behind,), device_id_type=MESH)

    @pl.when(has_ahead)
    def _():
        pl.semaphore_signal(barrier, inc=1, device_id=(ahead,), device_id_type=MESH)

    for load in loads:
        load.start()
    pl.semaphore_wait(
        barrier, 1 + has_behind.astype(jnp.int32) + has_ahead.astype(jnp.int32)
    )

    for step in range(steps):
        feat_copy(step, odd).start()

        @pl.when(is_odd & has_ahead)
        def _():
            past_copy_own(step).start()

        grad_copy(step, odd).start()

    @pl.when(jnp.logical_not(has_behind))
    def _():
        past[...] = jnp.zeros_like(past)

    @pl.when(jnp.logical_not(has_ahead))
    def _():
        far_in[...] = jnp.zeros_like(far_in)

    for load in loads:
        load.wait()

    def position(before, here, upstream):
        gates = jnp.dot(
            before, conv[:width], preferred_element_type=jnp.float32
        ) + jnp.dot(here, conv[width:], preferred_element_type=jnp.float32)
        tanh_part = jnp.tanh(gates[:, :width])
        sig_part = 0.5 * jnp.tanh(0.5 * gates[:, width:]) + 0.5
        d_mixed = contract_rows(upstream, proj[...])
        scaled = d_mixed * sig_part
        d_tanh = scaled * (1.0 - tanh_part * tanh_part)
        d_sig = scaled * tanh_part * (1.0 - sig_part)
        d_gates = jnp.concatenate(
            [d_tanh.astype(jnp.bfloat16), d_sig.astype(jnp.bfloat16)], 1
        )
        return contract_rows(d_gates, conv[:width]), contract_rows(d_gates, conv[width:])

    def finish(step):
        @pl.when(has_ahead)
        def _():
            far_copy(step).wait_recv()

        total = near_b[part(step)] + far_in[part(step)].astype(jnp.float32)

        @pl.when(is_even)
        def _():
            sum_out[part(step)] = total.astype(jnp.bfloat16)
            sum_copy(step).start()

        @pl.when(is_odd)
        def _():
            held[part(step, mine)] = grad[1, part(step)].astype(jnp.float32) + total
            store(step, mine, step).start()

    def body(step, carry):
        feat_copy(step, 1 - odd).wait_recv()

        @pl.when(is_even & has_ahead)
        def _():
            past_copy_on(step).start()

        @pl.when(is_odd)
        def _():
            grad_copy(step, 1 - odd).wait_recv()

        @pl.when(has_behind)
        def _():
            past_copy_own(step).wait_recv()

        far_a, near_a = position(
            past[part(step)], feat[0, part(step)], grad[0, part(step)]
        )
        far_out[part(step)] = far_a.astype(jnp.bfloat16)

        @pl.when(has_behind)
        def _():
            far_copy(step).start()

        @pl.when(is_even)
        def _():
            grad_copy(step, 1 - odd).wait_recv()

        far_b, nearer = position(
            feat[0, part(step)], feat[1, part(step)], grad[1, part(step)]
        )
        near_b[part(step)] = nearer
        total = near_a + far_b

        @pl.when(is_odd)
        def _():
            sum_out[part(step)] = total.astype(jnp.bfloat16)
            sum_copy(step).start()

        @pl.when(is_even)
        def _():
            held[part(step, mine)] = grad[0, part(step)].astype(jnp.float32) + total
            store(step, mine, step).start()

        @pl.when(step > 0)
        def _():
            finish(step - 1)

        return carry

    lax.fori_loop(0, steps, body, 0)
    finish(steps - 1)

    for step in range(steps):
        sum_copy(step).wait_recv()
        held[part(step, theirs)] = grad_home[part(step)].astype(jnp.float32) + sum_in[
            part(step)
        ].astype(jnp.float32)
        store(step, theirs, steps + step).start()

    for step in range(steps):
        feat_copy(step, odd).wait_send()
        grad_copy(step, odd).wait_send()
        sum_copy(step).wait_send()

        @pl.when(has_ahead)
        def _():
            past_copy_own(step).wait_send()

        @pl.when(has_behind)
        def _():
            far_copy(step).wait_send()

        store(step, mine, step).wait()
        store(step, theirs, steps + step).wait()


def shards(signal, grad_out, conv_weight, proj_weight):
    devices = lax.axis_size("seq")
    count, width = signal.shape
    half = count // 2
    narrow = pltpu.VMEM((half, width), jnp.bfloat16)
    pair = pltpu.VMEM((2, half, width), jnp.bfloat16)
    per_step = pltpu.SemaphoreType.DMA((STEPS,))
    return pl.pallas_call(
        functools.partial(kernel, devices, STEPS),
        out_shape=jax.ShapeDtypeStruct((count, width), jnp.float32),
        in_specs=[pl.BlockSpec(memory_space=pl.ANY)] * 4,
        out_specs=pl.BlockSpec(memory_space=pl.ANY),
        scratch_shapes=[
            pair, pair, narrow, narrow, narrow, narrow, narrow, narrow,
            pltpu.VMEM((half, width), jnp.float32),
            pltpu.VMEM((count, width), jnp.float32),
            pltpu.VMEM(conv_weight.shape, jnp.bfloat16),
            pltpu.VMEM(proj_weight.shape, jnp.bfloat16),
            pltpu.SemaphoreType.DMA((5,)),
        ] + [per_step] * 10 + [pltpu.SemaphoreType.DMA((2 * STEPS,))],
        compiler_params=pltpu.CompilerParams(
            collective_id=0, has_side_effects=True, vmem_limit_bytes=48 * 2**20
        ),
        cost_estimate=pl.CostEstimate(
            flops=2 * count * width * width * 9,
            bytes_accessed=16 * count * width,
            transcendentals=2 * count * width,
        ),
    )(signal, grad_out, conv_weight, proj_weight)


def solution(mesh):
    in_specs = (P("seq", None), P("seq", None), P(), P())
    out_specs = P("seq", None)
    return jax.shard_map(shards, mesh=mesh, in_specs=in_specs, out_specs=out_specs, check_vma=False)
```

```python
import functools

import jax
import jax.numpy as jnp
from jax import lax
from jax.experimental import pallas as pl
from jax.experimental.pallas import tpu as pltpu
from jax.sharding import PartitionSpec as P

MESH = pl.DeviceIdType.MESH
STEPS = 4


def contract_rows(left, right):
    return lax.dot_general(
        left, right, (((1,), (1,)), ((), ())), preferred_element_type=jnp.float32
    )


def kernel(
    devices, steps,
    signal_ref, grad_ref, conv_ref, proj_ref, out_ref,
    chain, grad, grad_home, far_in, far_out, sum_in, sum_out, near_b, held,
    conv, proj,
    load_sem, feat_send, feat_recv, grad_send, grad_recv, past_send, past_recv,
    far_send, far_recv, sum_send, sum_recv, store_sem,
):
    me = lax.axis_index("seq")
    odd = lax.rem(lax.div(me, 2), 2)
    partner = me + 2 - 4 * odd
    behind, ahead = me - 4, me + 4
    has_behind, has_ahead = me >= 4, me < devices - 4
    is_odd, is_even = odd == 1, odd == 0
    half, width = grad.shape[1:]
    rows = half // steps
    mine, theirs = odd * half, (1 - odd) * half

    def part(step, base=0):
        return pl.ds(pl.multiple_of(base + step * rows, rows), rows)

    def remote(src, dst, send, recv, target):
        return pltpu.make_async_remote_copy(
            src_ref=src, dst_ref=dst, send_sem=send, recv_sem=recv,
            device_id=(target,), device_id_type=MESH,
        )

    def feat_copy(step, slot):
        return remote(
            signal_ref.at[part(step, theirs)], chain.at[1 + slot, part(step)],
            feat_send.at[step], feat_recv.at[step], partner,
        )

    def grad_copy(step, slot):
        return remote(
            grad_ref.at[part(step, theirs)], grad.at[slot, part(step)],
            grad_send.at[step], grad_recv.at[step], partner,
        )

    def past_copy_own(step):
        return remote(
            signal_ref.at[part(step, mine)], chain.at[0, part(step)],
            past_send.at[step], past_recv.at[step], ahead,
        )

    def past_copy_on(step):
        return remote(
            chain.at[2, part(step)], chain.at[0, part(step)],
            past_send.at[step], past_recv.at[step], ahead,
        )

    def far_copy(step):
        return remote(
            far_out.at[part(step)], far_in.at[part(step)],
            far_send.at[step], far_recv.at[step], behind,
        )

    def sum_copy(step):
        return remote(
            sum_out.at[part(step)], sum_in.at[part(step)],
            sum_send.at[step], sum_recv.at[step], partner,
        )

    def store(step, base, index):
        return pltpu.make_async_copy(
            held.at[part(step, base)], out_ref.at[part(step, base)],
            store_sem.at[index],
        )

    loads = [
        pltpu.make_async_copy(src, dst, load_sem.at[i])
        for i, (src, dst) in enumerate([
            (conv_ref, conv),
            (proj_ref, proj),
            (signal_ref.at[pl.ds(pl.multiple_of(mine, half), half)], chain.at[1 + odd]),
            (grad_ref.at[pl.ds(pl.multiple_of(mine, half), half)], grad.at[odd]),
            (grad_ref.at[pl.ds(pl.multiple_of(theirs, half), half)], grad_home),
        ])
    ]

    barrier = pltpu.get_barrier_semaphore()
    pl.semaphore_signal(barrier, inc=1, device_id=(partner,), device_id_type=MESH)

    @pl.when(has_behind)
    def _():
        pl.semaphore_signal(barrier, inc=1, device_id=(behind,), device_id_type=MESH)

    @pl.when(has_ahead)
    def _():
        pl.semaphore_signal(barrier, inc=1, device_id=(ahead,), device_id_type=MESH)

    for load in loads:
        load.start()
    pl.semaphore_wait(
        barrier, 1 + has_behind.astype(jnp.int32) + has_ahead.astype(jnp.int32)
    )

    for step in range(steps):
        feat_copy(step, odd).start()

        @pl.when(is_odd & has_ahead)
        def _():
            past_copy_own(step).start()

        grad_copy(step, odd).start()

    @pl.when(jnp.logical_not(has_behind))
    def _():
        chain[0] = jnp.zeros((half, width), chain.dtype)

    @pl.when(jnp.logical_not(has_ahead))
    def _():
        far_in[...] = jnp.zeros_like(far_in)

    for load in loads:
        load.wait()

    def positions(before, here, upstream):
        gates = jnp.dot(
            before, conv[:width], preferred_element_type=jnp.float32
        ) + jnp.dot(here, conv[width:], preferred_element_type=jnp.float32)
        tanh_part = jnp.tanh(gates[:, :width])
        sig_part = 0.5 * jnp.tanh(0.5 * gates[:, width:]) + 0.5
        d_mixed = contract_rows(upstream, proj[...])
        scaled = d_mixed * sig_part
        d_tanh = scaled * (1.0 - tanh_part * tanh_part)
        d_sig = scaled * tanh_part * (1.0 - sig_part)
        d_gates = jnp.concatenate(
            [d_tanh.astype(jnp.bfloat16), d_sig.astype(jnp.bfloat16)], 1
        )
        return contract_rows(d_gates, conv[:width]), contract_rows(d_gates, conv[width:])

    def finish(step):
        @pl.when(has_ahead)
        def _():
            far_copy(step).wait_recv()

        total = near_b[part(step)] + far_in[part(step)].astype(jnp.float32)

        @pl.when(is_even)
        def _():
            sum_out[part(step)] = total.astype(jnp.bfloat16)

        @pl.when(is_odd)
        def _():
            held[part(step, mine)] = grad[1, part(step)].astype(jnp.float32) + total
            store(step, mine, step).start()

    def pass_on(step):
        feat_copy(step, 1 - odd).wait_recv()

        @pl.when(is_even & has_ahead)
        def _():
            past_copy_on(step).start()

    pass_on(0)

    def body(step, carry):
        @pl.when(step + 1 < steps)
        def _():
            pass_on(step + 1)

        grad_copy(step, 1 - odd).wait_recv()

        @pl.when(step > 1)
        def _():
            finish(step - 2)
            sum_copy(step - 2).start()


        @pl.when(has_behind)
        def _():
            past_copy_own(step).wait_recv()

        flat = (2 * rows, width)
        far, near = positions(
            chain[0:2, part(step)].reshape(flat),
            chain[1:3, part(step)].reshape(flat),
            grad[:, part(step)].reshape(flat),
        )
        far_out[part(step)] = far[:rows].astype(jnp.bfloat16)

        @pl.when(has_behind)
        def _():
            far_copy(step).start()

        near_b[part(step)] = near[rows:]
        total = near[:rows] + far[rows:]

        @pl.when(is_odd)
        def _():
            sum_out[part(step)] = total.astype(jnp.bfloat16)

        @pl.when(is_even)
        def _():
            held[part(step, mine)] = grad[0, part(step)].astype(jnp.float32) + total
            store(step, mine, step).start()

        return carry

    lax.fori_loop(0, steps, body, 0)

    for step in range(steps - 2, steps):
        @pl.when(is_odd)
        def _():
            sum_copy(step).start()

        finish(step)

        @pl.when(is_even)
        def _():
            sum_copy(step).start()

    for step in range(steps):
        sum_copy(step).wait_recv()
        held[part(step, theirs)] = grad_home[part(step)].astype(jnp.float32) + sum_in[
            part(step)
        ].astype(jnp.float32)
        store(step, theirs, steps + step).start()

    for step in range(steps):
        feat_copy(step, odd).wait_send()
        grad_copy(step, odd).wait_send()
        sum_copy(step).wait_send()

        @pl.when(has_ahead)
        def _():
            past_copy_own(step).wait_send()

        @pl.when(has_behind)
        def _():
            far_copy(step).wait_send()

        store(step, mine, step).wait()
        store(step, theirs, steps + step).wait()


def shards(signal, grad_out, conv_weight, proj_weight):
    devices = lax.axis_size("seq")
    count, width = signal.shape
    half = count // 2
    narrow = pltpu.VMEM((half, width), jnp.bfloat16)
    pair = pltpu.VMEM((2, half, width), jnp.bfloat16)
    per_step = pltpu.SemaphoreType.DMA((STEPS,))
    return pl.pallas_call(
        functools.partial(kernel, devices, STEPS),
        out_shape=jax.ShapeDtypeStruct((count, width), jnp.float32),
        in_specs=[pl.BlockSpec(memory_space=pl.ANY)] * 4,
        out_specs=pl.BlockSpec(memory_space=pl.ANY),
        scratch_shapes=[
            pltpu.VMEM((3, half, width), jnp.bfloat16),
            pair, narrow, narrow, narrow, narrow, narrow,
            pltpu.VMEM((half, width), jnp.float32),
            pltpu.VMEM((count, width), jnp.float32),
            pltpu.VMEM(conv_weight.shape, jnp.bfloat16),
            pltpu.VMEM(proj_weight.shape, jnp.bfloat16),
            pltpu.SemaphoreType.DMA((5,)),
        ] + [per_step] * 10 + [pltpu.SemaphoreType.DMA((2 * STEPS,))],
        compiler_params=pltpu.CompilerParams(
            collective_id=0, has_side_effects=True, vmem_limit_bytes=60 * 2**20
        ),
        cost_estimate=pl.CostEstimate(
            flops=2 * count * width * width * 9,
            bytes_accessed=16 * count * width,
            transcendentals=2 * count * width,
        ),
    )(signal, grad_out, conv_weight, proj_weight)


def solution(mesh):
    in_specs = (P("seq", None), P("seq", None), P(), P())
    out_specs = P("seq", None)
    return jax.shard_map(shards, mesh=mesh, in_specs=in_specs, out_specs=out_specs, check_vma=False)
```

```python
import functools

import jax
import jax.numpy as jnp
from jax import lax
from jax.experimental import pallas as pl
from jax.experimental.pallas import tpu as pltpu
from jax.sharding import PartitionSpec as P

MESH = pl.DeviceIdType.MESH
STEPS = 4


def contract_rows(left, right):
    return lax.dot_general(
        left, right, (((1,), (1,)), ((), ())), preferred_element_type=jnp.float32
    )


def kernel(
    devices, steps,
    signal_ref, grad_ref, conv_ref, proj_ref, out_ref,
    chain, grad, grad_home, far_in, far_out, sum_in, sum_out, near_b,
    conv, proj,
    load_sem, feat_send, feat_recv, grad_send, grad_recv, past_send, past_recv,
    far_send, far_recv, sum_send, sum_recv,
):
    me = lax.axis_index("seq")
    odd = lax.rem(lax.div(me, 2), 2)
    partner = me + 2 - 4 * odd
    behind, ahead = me - 4, me + 4
    has_behind, has_ahead = me >= 4, me < devices - 4
    is_odd, is_even = odd == 1, odd == 0
    half, width = grad.shape[1:]
    rows = half // steps
    mine, theirs = odd * half, (1 - odd) * half

    def part(step, base=0):
        return pl.ds(pl.multiple_of(base + step * rows, rows), rows)

    def remote(src, dst, send, recv, target):
        return pltpu.make_async_remote_copy(
            src_ref=src, dst_ref=dst, send_sem=send, recv_sem=recv,
            device_id=(target,), device_id_type=MESH,
        )

    def feat_copy(step, slot):
        return remote(
            signal_ref.at[part(step, theirs)], chain.at[1 + slot, part(step)],
            feat_send.at[step], feat_recv.at[step], partner,
        )

    def grad_copy(step, slot):
        return remote(
            grad_ref.at[part(step, theirs)], grad.at[slot, part(step)],
            grad_send.at[step], grad_recv.at[step], partner,
        )

    def past_copy_own(step):
        return remote(
            signal_ref.at[part(step, mine)], chain.at[0, part(step)],
            past_send.at[step], past_recv.at[step], ahead,
        )

    def past_copy_on(step):
        return remote(
            chain.at[2, part(step)], chain.at[0, part(step)],
            past_send.at[step], past_recv.at[step], ahead,
        )

    def far_copy(step):
        return remote(
            far_out.at[part(step)], far_in.at[part(step)],
            far_send.at[step], far_recv.at[step], behind,
        )

    def sum_copy(step):
        return remote(
            sum_out.at[part(step)], sum_in.at[part(step)],
            sum_send.at[step], sum_recv.at[step], partner,
        )

    loads = [
        pltpu.make_async_copy(src, dst, load_sem.at[i])
        for i, (src, dst) in enumerate([
            (conv_ref, conv),
            (proj_ref, proj),
            (signal_ref.at[pl.ds(pl.multiple_of(mine, half), half)], chain.at[1 + odd]),
            (grad_ref.at[pl.ds(pl.multiple_of(mine, half), half)], grad.at[odd]),
            (grad_ref.at[pl.ds(pl.multiple_of(theirs, half), half)], grad_home),
        ])
    ]

    barrier = pltpu.get_barrier_semaphore()
    pl.semaphore_signal(barrier, inc=1, device_id=(partner,), device_id_type=MESH)

    @pl.when(has_behind)
    def _():
        pl.semaphore_signal(barrier, inc=1, device_id=(behind,), device_id_type=MESH)

    @pl.when(has_ahead)
    def _():
        pl.semaphore_signal(barrier, inc=1, device_id=(ahead,), device_id_type=MESH)

    for load in loads:
        load.start()
    pl.semaphore_wait(
        barrier, 1 + has_behind.astype(jnp.int32) + has_ahead.astype(jnp.int32)
    )

    for step in range(steps):
        feat_copy(step, odd).start()

        @pl.when(is_odd & has_ahead)
        def _():
            past_copy_own(step).start()

        grad_copy(step, odd).start()

    @pl.when(jnp.logical_not(has_behind))
    def _():
        chain[0] = jnp.zeros((half, width), chain.dtype)

    @pl.when(jnp.logical_not(has_ahead))
    def _():
        far_in[...] = jnp.zeros_like(far_in)

    for load in loads:
        load.wait()

    def positions(before, here, upstream):
        gates = jnp.dot(
            before, conv[:width], preferred_element_type=jnp.float32
        ) + jnp.dot(here, conv[width:], preferred_element_type=jnp.float32)
        tanh_part = jnp.tanh(gates[:, :width])
        sig_part = 0.5 * jnp.tanh(0.5 * gates[:, width:]) + 0.5
        d_mixed = contract_rows(upstream, proj[...])
        scaled = d_mixed * sig_part
        d_tanh = scaled * (1.0 - tanh_part * tanh_part)
        d_sig = scaled * tanh_part * (1.0 - sig_part)
        d_gates = jnp.concatenate(
            [d_tanh.astype(jnp.bfloat16), d_sig.astype(jnp.bfloat16)], 1
        )
        return contract_rows(d_gates, conv[:width]), contract_rows(d_gates, conv[width:])

    def finish(step):
        @pl.when(has_ahead)
        def _():
            far_copy(step).wait_recv()

        total = near_b[part(step)] + far_in[part(step)].astype(jnp.float32)

        @pl.when(is_even)
        def _():
            sum_out[part(step)] = total.astype(jnp.bfloat16)

        @pl.when(is_odd)
        def _():
            out_ref[part(step, mine)] = grad[1, part(step)].astype(jnp.float32) + total

    def pass_on(step):
        feat_copy(step, 1 - odd).wait_recv()

        @pl.when(is_even & has_ahead)
        def _():
            past_copy_on(step).start()

    pass_on(0)

    def body(step, carry):
        @pl.when(step + 1 < steps)
        def _():
            pass_on(step + 1)

        grad_copy(step, 1 - odd).wait_recv()

        @pl.when(step > 1)
        def _():
            finish(step - 2)
            sum_copy(step - 2).start()


        @pl.when(has_behind)
        def _():
            past_copy_own(step).wait_recv()

        flat = (2 * rows, width)
        far, near = positions(
            chain[0:2, part(step)].reshape(flat),
            chain[1:3, part(step)].reshape(flat),
            grad[:, part(step)].reshape(flat),
        )
        far_out[part(step)] = far[:rows].astype(jnp.bfloat16)

        @pl.when(has_behind)
        def _():
            far_copy(step).start()

        near_b[part(step)] = near[rows:]
        total = near[:rows] + far[rows:]

        @pl.when(is_odd)
        def _():
            sum_out[part(step)] = total.astype(jnp.bfloat16)

        @pl.when(is_even)
        def _():
            out_ref[part(step, mine)] = grad[0, part(step)].astype(jnp.float32) + total

        return carry

    lax.fori_loop(0, steps, body, 0)

    for step in range(steps - 2, steps):
        @pl.when(is_odd)
        def _():
            sum_copy(step).start()

        finish(step)

        @pl.when(is_even)
        def _():
            sum_copy(step).start()

    for step in range(steps):
        sum_copy(step).wait_recv()
        out_ref[part(step, theirs)] = grad_home[part(step)].astype(jnp.float32) + sum_in[
            part(step)
        ].astype(jnp.float32)

    for step in range(steps):
        feat_copy(step, odd).wait_send()
        grad_copy(step, odd).wait_send()
        sum_copy(step).wait_send()

        @pl.when(has_ahead)
        def _():
            past_copy_own(step).wait_send()

        @pl.when(has_behind)
        def _():
            far_copy(step).wait_send()


def shards(signal, grad_out, conv_weight, proj_weight):
    devices = lax.axis_size("seq")
    count, width = signal.shape
    half = count // 2
    narrow = pltpu.VMEM((half, width), jnp.bfloat16)
    pair = pltpu.VMEM((2, half, width), jnp.bfloat16)
    per_step = pltpu.SemaphoreType.DMA((STEPS,))
    return pl.pallas_call(
        functools.partial(kernel, devices, STEPS),
        out_shape=pltpu.VMEM((count, width), jnp.float32),
        in_specs=[pl.BlockSpec(memory_space=pl.ANY)] * 4,
        out_specs=pl.BlockSpec(memory_space=pltpu.VMEM),
        scratch_shapes=[
            pltpu.VMEM((3, half, width), jnp.bfloat16),
            pair, narrow, narrow, narrow, narrow, narrow,
            pltpu.VMEM((half, width), jnp.float32),
            pltpu.VMEM(conv_weight.shape, jnp.bfloat16),
            pltpu.VMEM(proj_weight.shape, jnp.bfloat16),
            pltpu.SemaphoreType.DMA((5,)),
        ] + [per_step] * 10,
        compiler_params=pltpu.CompilerParams(
            collective_id=0, has_side_effects=True, vmem_limit_bytes=60 * 2**20
        ),
        cost_estimate=pl.CostEstimate(
            flops=2 * count * width * width * 9,
            bytes_accessed=16 * count * width,
            transcendentals=2 * count * width,
        ),
    )(signal, grad_out, conv_weight, proj_weight)


def solution(mesh):
    in_specs = (P("seq", None), P("seq", None), P(), P())
    out_specs = P("seq", None)
    return jax.shard_map(shards, mesh=mesh, in_specs=in_specs, out_specs=out_specs, check_vma=False)
```

```python
import functools

import jax
import jax.numpy as jnp
from jax import lax
from jax.experimental import pallas as pl
from jax.experimental.pallas import tpu as pltpu
from jax.sharding import PartitionSpec as P

MESH = pl.DeviceIdType.MESH
STEPS = 4


def contract_rows(left, right):
    return lax.dot_general(
        left, right, (((1,), (1,)), ((), ())), preferred_element_type=jnp.float32
    )


def kernel(
    devices, steps,
    signal_ref, grad_ref, conv_ref, proj_ref, out_ref,
    chain, grad, grad_home, far_in, far_out, sum_in, sum_out, near_b,
    conv, proj,
    load_sem, feat_send, feat_recv, grad_send, grad_recv, past_send, past_recv,
    far_send, far_recv, sum_send, sum_recv,
):
    me = lax.axis_index("seq")
    odd = lax.rem(lax.div(me, 2), 2)
    partner = me + 2 - 4 * odd
    behind, ahead = me - 4, me + 4
    has_behind, has_ahead = me >= 4, me < devices - 4
    is_odd, is_even = odd == 1, odd == 0
    half, width = grad.shape[1:]
    rows = half // steps
    mine, theirs = odd * half, (1 - odd) * half

    def part(step, base=0):
        return pl.ds(pl.multiple_of(base + step * rows, rows), rows)

    def remote(src, dst, send, recv, target):
        return pltpu.make_async_remote_copy(
            src_ref=src, dst_ref=dst, send_sem=send, recv_sem=recv,
            device_id=(target,), device_id_type=MESH,
        )

    def feat_copy(step, slot):
        return remote(
            signal_ref.at[part(step, theirs)], chain.at[1 + slot, part(step)],
            feat_send.at[step], feat_recv.at[step], partner,
        )

    def grad_copy(step, slot):
        return remote(
            grad_ref.at[part(step, theirs)], grad.at[slot, part(step)],
            grad_send.at[step], grad_recv.at[step], partner,
        )

    def past_copy_own(step):
        return remote(
            signal_ref.at[part(step, mine)], chain.at[0, part(step)],
            past_send.at[step], past_recv.at[step], ahead,
        )

    def past_copy_on(step):
        return remote(
            chain.at[2, part(step)], chain.at[0, part(step)],
            past_send.at[step], past_recv.at[step], ahead,
        )

    def far_copy(step):
        return remote(
            far_out.at[part(step)], far_in.at[part(step)],
            far_send.at[step], far_recv.at[step], behind,
        )

    def sum_copy(step):
        return remote(
            sum_out.at[part(step)], sum_in.at[part(step)],
            sum_send.at[step], sum_recv.at[step], partner,
        )

    loads = [
        pltpu.make_async_copy(src, dst, load_sem.at[i])
        for i, (src, dst) in enumerate([
            (conv_ref, conv),
            (proj_ref, proj),
            (signal_ref.at[pl.ds(pl.multiple_of(mine, half), half)], chain.at[1 + odd]),
            (grad_ref.at[pl.ds(pl.multiple_of(mine, half), half)], grad.at[odd]),
            (grad_ref.at[pl.ds(pl.multiple_of(theirs, half), half)], grad_home),
        ])
    ]

    barrier = pltpu.get_barrier_semaphore()
    pl.semaphore_signal(barrier, inc=1, device_id=(partner,), device_id_type=MESH)

    @pl.when(has_behind)
    def _():
        pl.semaphore_signal(barrier, inc=1, device_id=(behind,), device_id_type=MESH)

    @pl.when(has_ahead)
    def _():
        pl.semaphore_signal(barrier, inc=1, device_id=(ahead,), device_id_type=MESH)

    for load in loads:
        load.start()
    pl.semaphore_wait(
        barrier, 1 + has_behind.astype(jnp.int32) + has_ahead.astype(jnp.int32)
    )

    for step in range(steps):
        feat_copy(step, odd).start()

        @pl.when(is_odd & has_ahead)
        def _():
            past_copy_own(step).start()

        grad_copy(step, odd).start()

    @pl.when(jnp.logical_not(has_behind))
    def _():
        chain[0] = jnp.zeros((half, width), chain.dtype)

    @pl.when(jnp.logical_not(has_ahead))
    def _():
        far_in[...] = jnp.zeros_like(far_in)

    for load in loads:
        load.wait()

    def positions(before, here, upstream):
        gates = jnp.dot(
            before, conv[:width], preferred_element_type=jnp.float32
        ) + jnp.dot(here, conv[width:], preferred_element_type=jnp.float32)
        tanh_part = jnp.tanh(gates[:, :width])
        sig_part = 0.5 * jnp.tanh(0.5 * gates[:, width:]) + 0.5
        d_mixed = contract_rows(upstream, proj[...])
        scaled = d_mixed * sig_part
        d_tanh = scaled * (1.0 - tanh_part * tanh_part)
        d_sig = scaled * tanh_part * (1.0 - sig_part)
        d_gates = jnp.concatenate(
            [d_tanh.astype(jnp.bfloat16), d_sig.astype(jnp.bfloat16)], 1
        )
        return contract_rows(d_gates, conv[:width]), contract_rows(d_gates, conv[width:])

    def finish(step):
        @pl.when(has_ahead)
        def _():
            far_copy(step).wait_recv()

        total = near_b[part(step)] + far_in[part(step)].astype(jnp.float32)

        @pl.when(is_even)
        def _():
            sum_out[part(step)] = total.astype(jnp.bfloat16)

        @pl.when(is_odd)
        def _():
            out_ref[part(step, mine)] = grad[1, part(step)].astype(jnp.float32) + total

    def pass_on(step):
        feat_copy(step, 1 - odd).wait_recv()

        @pl.when(is_even & has_ahead)
        def _():
            past_copy_on(step).start()

    pass_on(0)

    def body(step, carry):
        @pl.when(step + 1 < steps)
        def _():
            pass_on(step + 1)

        grad_copy(step, 1 - odd).wait_recv()


        @pl.when(has_behind)
        def _():
            past_copy_own(step).wait_recv()

        far_a, near_a = positions(
            chain[0, part(step)], chain[1, part(step)], grad[0, part(step)]
        )
        far_out[part(step)] = far_a.astype(jnp.bfloat16)

        @pl.when(has_behind)
        def _():
            far_copy(step).start()

        far_b, nearer = positions(
            chain[1, part(step)], chain[2, part(step)], grad[1, part(step)]
        )
        near_b[part(step)] = nearer
        total = near_a + far_b

        @pl.when(is_odd)
        def _():
            sum_out[part(step)] = total.astype(jnp.bfloat16)
            sum_copy(step).start()

        @pl.when(is_even)
        def _():
            out_ref[part(step, mine)] = grad[0, part(step)].astype(jnp.float32) + total

        @pl.when(step > 0)
        def _():
            finish(step - 1)

            @pl.when(is_even)
            def _():
                sum_copy(step - 1).start()

        return carry

    lax.fori_loop(0, steps, body, 0)

    for step in range(steps - 1, steps):
        finish(step)

        @pl.when(is_even)
        def _():
            sum_copy(step).start()

    for step in range(steps):
        sum_copy(step).wait_recv()
        out_ref[part(step, theirs)] = grad_home[part(step)].astype(jnp.float32) + sum_in[
            part(step)
        ].astype(jnp.float32)

    for step in range(steps):
        feat_copy(step, odd).wait_send()
        grad_copy(step, odd).wait_send()
        sum_copy(step).wait_send()

        @pl.when(has_ahead)
        def _():
            past_copy_own(step).wait_send()

        @pl.when(has_behind)
        def _():
            far_copy(step).wait_send()


def shards(signal, grad_out, conv_weight, proj_weight):
    devices = lax.axis_size("seq")
    count, width = signal.shape
    half = count // 2
    narrow = pltpu.VMEM((half, width), jnp.bfloat16)
    pair = pltpu.VMEM((2, half, width), jnp.bfloat16)
    per_step = pltpu.SemaphoreType.DMA((STEPS,))
    return pl.pallas_call(
        functools.partial(kernel, devices, STEPS),
        out_shape=pltpu.VMEM((count, width), jnp.float32),
        in_specs=[pl.BlockSpec(memory_space=pl.ANY)] * 4,
        out_specs=pl.BlockSpec(memory_space=pltpu.VMEM),
        scratch_shapes=[
            pltpu.VMEM((3, half, width), jnp.bfloat16),
            pair, narrow, narrow, narrow, narrow, narrow,
            pltpu.VMEM((half, width), jnp.float32),
            pltpu.VMEM(conv_weight.shape, jnp.bfloat16),
            pltpu.VMEM(proj_weight.shape, jnp.bfloat16),
            pltpu.SemaphoreType.DMA((5,)),
        ] + [per_step] * 10,
        compiler_params=pltpu.CompilerParams(
            collective_id=0, has_side_effects=True, vmem_limit_bytes=60 * 2**20
        ),
        cost_estimate=pl.CostEstimate(
            flops=2 * count * width * width * 9,
            bytes_accessed=16 * count * width,
            transcendentals=2 * count * width,
        ),
    )(signal, grad_out, conv_weight, proj_weight)


def solution(mesh):
    in_specs = (P("seq", None), P("seq", None), P(), P())
    out_specs = P("seq", None)
    return jax.shard_map(shards, mesh=mesh, in_specs=in_specs, out_specs=out_specs, check_vma=False)
```
